32 devices in a mesh: row: 8 (over z, x), col: 4 (over y, core).
Axes of the slice: x: 2, y: 2, z: 4, core: 2. Of those that a mesh axis runs over, the one named last changes fastest.
Arguments:
- integrals: bfloat16 [16384, 4096], P('row', 'col'), may hold values from -0.046875 to 0.046875
- lambda2: bfloat16 [2016, 16384], P('col', 'row'), may hold values from -6 to 6
- source_terms: float32 [2016, 4096], P('row', 'col'), may hold values from -6 to 6
- hist_amp: bfloat16 [5, 2016, 4096], P(None, 'row', 'col'), may hold values from -6 to 6
- hist_err: bfloat16 [5, 2016, 4096], P(None, 'row', 'col'), may hold values from -64 to 64
- eps_occ: float32 [64], replicated, may hold values from -1 to -0.3
- eps_vir: float32 [800], replicated, may hold values from 0.1 to 1
- occ_pair: int32 [2, 2016], P(None, 'row'), may hold values from 0 to 63, as said below
- vir_pair: int32 [2, 4096], P(None, 'col'), may hold values from 0 to 799, as said below
Outputs:
- updated: float32 [2016, 4096], P('row', 'col')
The draws below stay inside these ranges and needn't reach their ends.
Inputs may be any that keep to these rules, and one draw needn't show every extreme that they name: `occ_pair`: every pair i < j of the 64 occupied orbitals appears exactly once, in some order. `vir_pair`: in every column the first orbital is smaller than the second.
All inputs are finite; a program needn't handle non-finite values.
Results may differ from the reference program's by a relative error of at most 0.0003.
Values may be sent and summed in bfloat16 or wider, within the bound.
No kernel may reach another device: no remote copies, remote signals or barrier semaphores. Data moves between devices by JAX's collectives and lax.ppermute only.
A program may use at most 64 MiB of HBM per device.

```python
import math
import jax
import jax.numpy as jnp
import numpy as np
from jax import lax

NOCC = 64
NVIR = 800
IJ = 2016
NHIST = 5
CD = 16384
AB = 4096


def draw_occ_pair(key, part):
    pairs = np.triu_indices(NOCC, 1)
    table = jnp.asarray(np.stack(pairs).astype(np.int32))
    order = jax.random.permutation(key, IJ)
    return table[:, order].astype(jnp.int32)


def draw_vir_pair(key, part):
    first_key, second_key = jax.random.split(jax.random.fold_in(key, 17))
    lower = jax.random.randint(first_key, (AB,), 0, NVIR - 1, dtype=jnp.int32)
    offsets = jax.random.randint(second_key, (AB,), 0, 1 << 20, dtype=jnp.int32)
    upper = lower + 1 + offsets % (NVIR - 1 - lower)
    return jnp.stack([lower, upper]).astype(jnp.int32)


def draw_hist_err(key, part):
    keys = jax.random.split(jax.random.fold_in(key, 29), 4)
    row_pos = jnp.arange(IJ, dtype=jnp.float32) / IJ
    col_pos = jnp.arange(AB, dtype=jnp.float32) / AB
    row_scale = jnp.exp(jax.random.uniform(keys[0], (IJ,), jnp.float32) * math.log(10.0)) * (1.0 + 2.0 * row_pos) / 8.0
    col_scale = jnp.exp(jax.random.uniform(keys[1], (AB,), jnp.float32) * math.log(10.0)) * (1.0 + 2.0 * col_pos) / 8.0
    common = jnp.clip(jax.random.normal(keys[2], (IJ, AB), jnp.float32), -6.0, 6.0)
    own = jnp.clip(jax.random.normal(keys[3], (NHIST, IJ, AB), jnp.float32), -6.0, 6.0)
    mixing = 0.6
    level = 1.2
    values = (mixing * common[None] + math.sqrt(1.0 - mixing * mixing) * own) * (row_scale[:, None] * col_scale[None, :])[None]
    return jnp.clip(level * values, -64.0, 64.0).astype(jnp.bfloat16)


def spiked(entries, stream_key, source, target, shards_of, factor):
    owner, partner = [(jnp.arange(entries.shape[dim]) // (entries.shape[dim] // shards_of)).reshape([-1 if axis == dim else 1 for axis in range(entries.ndim)]) for dim in (source, target)]
    chosen = jax.random.permutation(stream_key, shards_of)[partner]
    strong = (owner == chosen) | (owner == (partner + shards_of // 2) % shards_of)
    return jnp.where(strong, factor * entries, entries)


def level_of(own_key, dims, cuts, smallest, top_value):
    level, own = 1.0, jax.random.fold_in(own_key, 6)
    for dim, parts in cuts:
        steps = jnp.exp(jax.random.uniform(jax.random.fold_in(own, dim), (parts,), jnp.float32, smallest / len(cuts), top_value / len(cuts)))
        level = level * jnp.repeat(steps, dims[dim] // parts).reshape([-1 if axis == dim else 1 for axis in range(len(dims))])
    return level


def scatter_about(stream_key, shape, deviation, limit, cuts=(), kind=jnp.bfloat16):
    entries = deviation * jax.random.normal(stream_key, shape, jnp.float32)
    if cuts:
        entries = entries * level_of(stream_key, shape, cuts, -0.22, 0.18)
    return jnp.clip(entries, -limit, limit).astype(kind)


def gaussian_with(key, dims, scale, limit, cuts, heavy, kind=jnp.bfloat16):
    entries = scale * jax.random.normal(key, dims, jnp.float32)
    if cuts:
        entries = entries * level_of(key, dims, cuts, -0.22, 0.18)
    return jnp.clip(spiked(entries, jax.random.fold_in(key, 3), *heavy), -limit, limit).astype(kind)


def setup_inputs(seed: int = 0) -> dict:
    key_of = jax.random.split(jax.random.key(seed), 10)
    integrals = scatter_about(key_of[0], (CD, AB), CD ** -0.5, 0.046875, ((0, 8), (1, 4)))
    lambda2 = gaussian_with(key_of[1], (IJ, CD), 1.0, 6.0, ((0, 4), (1, 8)), (1, 0, 8, 2.0))
    source_terms = scatter_about(key_of[2], (IJ, AB), 1.0, 6.0, ((0, 8), (1, 4)), jnp.float32)
    hist_amp = scatter_about(key_of[3], (NHIST, IJ, AB), 1.0, 6.0, ((1, 8), (2, 4)))
    hist_err = draw_hist_err(jax.random.fold_in(key_of[9], 71), 0)
    eps_occ = jnp.clip(jax.random.uniform(key_of[5], (NOCC,), jnp.float32, -1.0, -0.3), -1.0, -0.3)
    eps_vir = jnp.clip(jax.random.uniform(key_of[6], (NVIR,), jnp.float32, 0.1, 1.0), 0.1, 1.0)
    occ_pair = draw_occ_pair(jax.random.fold_in(key_of[9], 71), 0)
    vir_pair = draw_vir_pair(jax.random.fold_in(key_of[9], 71), 0)
    return {"integrals": integrals, "lambda2": lambda2, "source_terms": source_terms, "hist_amp": hist_amp, "hist_err": hist_err, "eps_occ": eps_occ, "eps_vir": eps_vir, "occ_pair": occ_pair, "vir_pair": vir_pair}


precise = lax.Precision.HIGHEST

def pair_energy(pairs, energies):
    levels = jnp.arange(energies.shape[0], dtype=jnp.int32)
    first = jnp.sum(jnp.where(pairs[0][:, None] == levels[None, :], energies[None, :], 0.0), axis=1)
    second = jnp.sum(jnp.where(pairs[1][:, None] == levels[None, :], energies[None, :], 0.0), axis=1)
    return first + second

def diis_weights(correlation):
    factor = jnp.linalg.cholesky(correlation)
    order = correlation.shape[0]
    forward = []
    for k in range(order):
        running = jnp.ones((), correlation.dtype)
        for m in range(k):
            running = running - factor[k, m] * forward[m]
        forward.append(running / factor[k, k])
    backward = [None] * order
    for k in reversed(range(order)):
        running = forward[k]
        for m in range(k + 1, order):
            running = running - factor[m, k] * backward[m]
        backward[k] = running / factor[k, k]
    solved = jnp.stack(backward)
    return solved / jnp.sum(solved)

def reference(integrals, lambda2, source_terms, hist_amp, hist_err, eps_occ, eps_vir, occ_pair, vir_pair):
    ladder = jnp.dot(lambda2.astype(jnp.float32), integrals.astype(jnp.float32), preferred_element_type=jnp.float32)
    denominator = pair_energy(occ_pair, eps_occ)[:, None] - pair_energy(vir_pair, eps_vir)[None, :]
    raw_update = (source_terms + ladder) / denominator
    err_new = raw_update - hist_amp[0].astype(jnp.float32)
    stored_count = hist_err.shape[0]
    stacked = jnp.concatenate([hist_err.astype(jnp.float32).reshape(stored_count, -1), err_new.reshape(1, -1)], axis=0)
    correlation = jnp.dot(stacked, stacked.T, precision=precise)
    weights = diis_weights(correlation)
    updated = weights[stored_count] * raw_update
    for k in range(stored_count):
        updated = updated + weights[k] * hist_amp[k].astype(jnp.float32)
    return updated
```

```python
import jax
import jax.numpy as jnp
from jax import lax
from jax.experimental import pallas as pl
from jax.experimental.pallas import tpu as pltpu
from jax.sharding import PartitionSpec as P

f32 = jnp.float32
wire = jnp.float16


def pair_energy(pairs, energies):
    levels = jnp.arange(energies.shape[0], dtype=jnp.int32)
    first = jnp.sum(jnp.where(pairs[0][:, None] == levels[None, :], energies[None, :], 0.0), axis=1)
    second = jnp.sum(
        jnp.where(pairs[1][:, None] == levels[None, :], energies[None, :], 0.0), axis=1
    )
    return first + second


def row_steps(rows, step, width, count, term):
    whole = rows // step

    def body(i, acc):
        parts = term(pl.ds(pl.multiple_of(i * step, step), step))
        return tuple(a + jnp.sum(p.reshape(step // 8, 8, width), axis=0) for a, p in zip(acc, parts))

    acc = lax.fori_loop(
        0, whole, body, tuple(jnp.zeros((8, width), f32) for _ in range(count))
    )
    sums = [jnp.sum(a, axis=0, keepdims=True) for a in acc]
    if rows % step:
        parts = term(pl.ds(whole * step, rows % step))
        sums = [s + jnp.sum(p, axis=0, keepdims=True) for s, p in zip(sums, parts)]
    return sums


def column_block(width):
    return 256 if width % 256 == 0 else width


def stored_products(hist_err):
    count, rows, width = hist_err.shape
    block = column_block(width)
    pairs = [(k, m) for k in range(count) for m in range(k + 1)]

    def kernel(err_ref, out_ref):
        def term(at):
            e = [err_ref[k, at, :].astype(f32) for k in range(count)]
            return [e[k] * e[m] for k, m in pairs]

        out_ref[...] = jnp.zeros_like(out_ref)
        for n, s in enumerate(row_steps(rows, 16, block, len(pairs), term)):
            out_ref[n : n + 1, :] = s

    padded = -(-len(pairs) // 8) * 8
    return pl.pallas_call(
        kernel,
        grid=(width // block,),
        in_specs=[pl.BlockSpec((count, rows, block), lambda i: (0, 0, i))],
        out_specs=pl.BlockSpec((padded, block), lambda i: (0, i)),
        out_shape=jax.ShapeDtypeStruct((padded, width), f32),
        cost_estimate=pl.CostEstimate(
            flops=2 * 15 * rows * width, bytes_accessed=hist_err.size * 2, transcendentals=0
        ),
    )(hist_err)


def new_products(ladder, source_terms, occ_energy, vir_energy, hist_amp, hist_err):
    count, rows, width = hist_err.shape
    block = column_block(width)

    def kernel(lad_ref, src_ref, occ_ref, vir_ref, amp_ref, err_ref, raw_ref, out_ref):
        def term(at):
            n = at.size
            den = occ_ref[at, 0:1] - vir_ref[...]
            raw = (src_ref[at, :] + lad_ref[at, :]) / den
            raw_ref[at, :] = raw
            new = raw - amp_ref[0, at, :].astype(f32)
            return [err_ref[k, at, :].astype(f32) * new for k in range(count)] + [new * new]

        out_ref[...] = jnp.zeros_like(out_ref)
        for n, s in enumerate(row_steps(rows, 16, block, count + 1, term)):
            out_ref[n : n + 1, :] = s

    columns = lambda i: (0, i)
    return pl.pallas_call(
        kernel,
        grid=(width // block,),
        in_specs=[
            pl.BlockSpec((rows, block), columns),
            pl.BlockSpec((rows, block), columns),
            pl.BlockSpec((rows, 128), lambda i: (0, 0)),
            pl.BlockSpec((1, block), columns),
            pl.BlockSpec((1, rows, block), lambda i: (0, 0, i)),
            pl.BlockSpec((count, rows, block), lambda i: (0, 0, i)),
        ],
        out_specs=[pl.BlockSpec((rows, block), columns), pl.BlockSpec((8, block), columns)],
        out_shape=[
            jax.ShapeDtypeStruct((rows, width), f32),
            jax.ShapeDtypeStruct((8, width), f32),
        ],
        cost_estimate=pl.CostEstimate(
            flops=20 * rows * width, bytes_accessed=hist_err.size * 2 + 14 * rows * width, transcendentals=0
        ),
    )(ladder, source_terms, occ_energy, vir_energy, hist_amp, hist_err)


def extrapolate(gathered, raw, hist_amp):
    count, rows, width = hist_amp.shape
    order = count + 1
    block = column_block(width)

    def kernel(sum_ref, raw_ref, amp_ref, out_ref):
        totals = jnp.sum(sum_ref[...], axis=0)
        lanes = lax.broadcasted_iota(jnp.int32, totals.shape, 1)
        subs = lax.broadcasted_iota(jnp.int32, totals.shape, 0)
        corr = {}
        n = 0
        for k in range(order):
            for m in range(k + 1):
                hit = (lanes == n) & (subs == 0)
                corr[k, m] = jnp.sum(jnp.where(hit, totals, 0.0), keepdims=True)
                n += 1
        factor = {}
        for m in range(order):
            diag = corr[m, m]
            for j in range(m):
                diag = diag - factor[m, j] * factor[m, j]
            factor[m, m] = jnp.sqrt(diag)
            for k in range(m + 1, order):
                value = corr[k, m]
                for j in range(m):
                    value = value - factor[k, j] * factor[m, j]
                factor[k, m] = value / factor[m, m]
        forward = []
        for k in range(order):
            running = jnp.ones((1, 1), f32)
            for m in range(k):
                running = running - factor[k, m] * forward[m]
            forward.append(running / factor[k, k])
        backward = [None] * order
        for k in reversed(range(order)):
            running = forward[k]
            for m in range(k + 1, order):
                running = running - factor[m, k] * backward[m]
            backward[k] = running / factor[k, k]
        whole = backward[0]
        for k in range(1, order):
            whole = whole + backward[k]
        weights = [b / whole for b in backward]
        updated = weights[count] * raw_ref[...]
        for k in range(count):
            updated = updated + weights[k] * amp_ref[k].astype(f32)
        out_ref[...] = updated

    columns = lambda i: (0, i)
    return pl.pallas_call(
        kernel,
        grid=(width // block,),
        in_specs=[
            pl.BlockSpec(gathered.shape, lambda i: (0, 0, 0)),
            pl.BlockSpec((rows, block), columns),
            pl.BlockSpec((count, rows, block), lambda i: (0, 0, i)),
        ],
        out_specs=pl.BlockSpec((rows, block), columns),
        out_shape=jax.ShapeDtypeStruct((rows, width), f32),
    )(gathered, raw, hist_amp)


def cuts_of(rows):
    step = max(16, -(-rows // 64) * 16)
    return [(at, min(step, rows - at)) for at in range(0, rows, step)]


def make(mesh):
    row_n, col_n = mesh.shape["row"], mesh.shape["col"]
    total = row_n * col_n

    def send_col(x, m):
        return lax.ppermute(x, "col", [(i, i ^ m) for i in range(col_n)])

    def send_row(x, m):
        return lax.ppermute(x, "row", [(i, i ^ m) for i in range(row_n)])

    def on_device(
        integrals, lambda2, source_terms, hist_amp, hist_err, eps_occ, eps_vir, occ_pair, vir_pair
    ):
        rows, width = source_terms.shape
        depth = lambda2.shape[1]
        near = lambda2.shape[0] // rows
        r, c = lax.axis_index("row"), lax.axis_index("col")
        zi = r // near
        low = lax.rem(zi, 2) == lax.rem(c, 2)

        def multiply(piece):
            out = jnp.dot(
                piece.reshape(-1, depth), integrals, preferred_element_type=f32
            )
            return out.reshape(near, -1, width)

        def over_near(part):
            bit = 1
            while part.shape[0] > 1:
                halves = part.reshape(part.shape[0] // 2, 2, *part.shape[1:])
                mine = (r // bit) % 2 == 0
                send = jnp.where(mine, halves[:, 1], halves[:, 0])
                keep = jnp.where(mine, halves[:, 0], halves[:, 1])
                part = keep + send_row(send.astype(wire), bit).astype(f32)
                bit *= 2
            return part[0]

        def over_pair(first, second):
            send = jnp.where(low, second, first)
            keep = jnp.where(low, first, second)
            return keep + send_row(send.astype(wire), near).astype(f32)

        def over_far(part, pair):
            kept = jnp.where(zi // 2 == (c // 2) ^ pair, part, 0.0)
            data = part.astype(wire)
            for d in range(1, col_n // 2):
                links = []
                for z in range(col_n):
                    for y in range(col_n):
                        if (z // 2) ^ (y // 2) ^ pair == d:
                            for x in range(near):
                                source = (z * near + x) * col_n + y
                                target = ((z ^ (2 * d)) * near + x) * col_n + y
                                links.append((source, target))
                kept = kept + lax.ppermute(data, ("row", "col"), links).astype(f32)
            return kept

        own = lambda2.reshape(near, rows, depth)
        cuts = cuts_of(rows)
        pieces = [own[:, at : at + size] for at, size in cuts]
        far = {
            (m, q): send_col(piece, m)
            for m in range(2, col_n, 2)
            for q, piece in enumerate(pieces)
        }
        sibling = send_col(own, 1)
        part = over_pair(over_near(multiply(own)), over_near(multiply(sibling)))
        ladder = over_far(part, 0)
        for m in range(2, col_n, 2):
            done = []
            for q in range(len(cuts)):
                other = send_col(far[m, q], 1)
                part = over_pair(
                    over_near(multiply(far[m, q])), over_near(multiply(other))
                )
                done.append(over_far(part, m // 2))
            ladder = ladder + jnp.concatenate(done, axis=0)

        occ_energy = jnp.broadcast_to(pair_energy(occ_pair, eps_occ)[:, None], (rows, 128))
        vir_energy = pair_energy(vir_pair, eps_vir)[None, :]
        stored = stored_products(hist_err)
        raw, fresh = new_products(
            ladder, source_terms, occ_energy, vir_energy, hist_amp, hist_err
        )
        count = hist_err.shape[0]
        pairs = count * (count + 1) // 2
        sums = jnp.concatenate(
            [jnp.sum(stored, axis=1)[:pairs], jnp.sum(fresh, axis=1)[: count + 1]]
        )
        tile = jnp.zeros((8, 128), f32).at[0, : sums.shape[0]].set(sums)
        gathered = lax.all_to_all(
            jnp.broadcast_to(tile[None], (total, 8, 128)), ("row", "col"), 0, 0, tiled=True
        )
        return extrapolate(gathered, raw, hist_amp)

    return on_device


def solution(mesh):
    placed = (
        P("row", "col"),
        P("col", "row"),
        P("row", "col"),
        P(None, "row", "col"),
        P(None, "row", "col"),
        P(),
        P(),
        P(None, "row"),
        P(None, "col"),
    )
    return jax.shard_map(
        make(mesh), mesh=mesh, in_specs=placed, out_specs=P("row", "col"), check_vma=False
    )
```

```python
import jax
import jax.numpy as jnp
from jax import lax
from jax.experimental import pallas as pl
from jax.experimental.pallas import tpu as pltpu
from jax.sharding import PartitionSpec as P

f32 = jnp.float32
wire = jnp.float16


def pair_energy(pairs, energies):
    levels = jnp.arange(energies.shape[0], dtype=jnp.int32)
    first = jnp.sum(jnp.where(pairs[0][:, None] == levels[None, :], energies[None, :], 0.0), axis=1)
    second = jnp.sum(
        jnp.where(pairs[1][:, None] == levels[None, :], energies[None, :], 0.0), axis=1
    )
    return first + second


def row_steps(rows, step, width, count, term):
    whole = rows // step

    def body(i, acc):
        parts = term(pl.ds(pl.multiple_of(i * step, step), step))
        return tuple(a + jnp.sum(p.reshape(step // 8, 8, width), axis=0) for a, p in zip(acc, parts))

    acc = tuple(jnp.zeros((8, width), f32) for _ in range(count))
    if whole:
        acc = lax.fori_loop(0, whole, body, acc, unroll=min(whole, 5))
    sums = [jnp.sum(a, axis=0, keepdims=True) for a in acc]
    if rows % step:
        parts = term(pl.ds(whole * step, rows % step))
        sums = [s + jnp.sum(p, axis=0, keepdims=True) for s, p in zip(sums, parts)]
    return sums


def column_block(width):
    return 256 if width % 256 == 0 else width


def padded(count):
    return -(-count // 8) * 8


def stored_products(hist_err):
    count, rows, width = hist_err.shape
    block = column_block(width)
    pairs = [(k, m) for k in range(count) for m in range(k + 1)]

    def kernel(err_ref, out_ref):
        def term(at):
            e = [err_ref[k, at, :].astype(f32) for k in range(count)]
            return [e[k] * e[m] for k, m in pairs]

        out_ref[...] = jnp.zeros_like(out_ref)
        for n, s in enumerate(row_steps(rows, 16, block, len(pairs), term)):
            out_ref[n : n + 1, :] = s

    return pl.pallas_call(
        kernel,
        grid=(width // block,),
        in_specs=[pl.BlockSpec((count, rows, block), lambda i: (0, 0, i))],
        out_specs=pl.BlockSpec((padded(len(pairs)), block), lambda i: (0, i)),
        out_shape=jax.ShapeDtypeStruct((padded(len(pairs)), width), f32),
        cost_estimate=pl.CostEstimate(
            flops=2 * len(pairs) * rows * width,
            bytes_accessed=hist_err.size * 2,
            transcendentals=0,
        ),
    )(hist_err)


def new_products(ladder, source_terms, occ_energy, vir_energy, hist_amp, hist_err, stored, copies):
    count, rows, width = hist_err.shape
    block = column_block(width)
    grid = width // block
    pairs = count * (count + 1) // 2
    fresh_at = stored.shape[0]

    def kernel(
        lad_ref, src_ref, occ_ref, vir_ref, amp_ref, err_ref, sto_ref, raw_ref, out_ref, sum_ref
    ):
        step = pl.program_id(0)

        @pl.when(step == 0)
        def _():
            sum_ref[...] = jnp.zeros_like(sum_ref)

        def term(at):
            den = occ_ref[at, 0:1] - vir_ref[...]
            raw = (src_ref[at, :] + lad_ref[at, :]) / den
            raw_ref[at, :] = raw
            new = raw - amp_ref[0, at, :].astype(f32)
            return [err_ref[k, at, :].astype(f32) * new for k in range(count)] + [new * new]

        sum_ref[0:fresh_at, :] += sto_ref[...]
        for n, s in enumerate(row_steps(rows, 16, block, count + 1, term)):
            sum_ref[fresh_at + n : fresh_at + n + 1, :] += s

        @pl.when(step == grid - 1)
        def _():
            column = jnp.sum(sum_ref[...], axis=1, keepdims=True)
            shape = (sum_ref.shape[0], 128)
            lane = lax.broadcasted_iota(jnp.int32, shape, 1)
            item = lax.broadcasted_iota(jnp.int32, shape, 0)
            place = jnp.where(item < fresh_at, item, item - fresh_at + pairs)
            used = (item < pairs) | (item >= fresh_at)
            spread = jnp.where((lane == place) & used, column, 0.0)
            out_ref[...] = jnp.broadcast_to(
                jnp.sum(spread, axis=0, keepdims=True), out_ref.shape
            )

    columns = lambda i: (0, i)
    return pl.pallas_call(
        kernel,
        grid=(grid,),
        in_specs=[
            pl.BlockSpec((ladder.shape[0], block), columns),
            pl.BlockSpec((rows, block), columns),
            pl.BlockSpec((rows, 128), lambda i: (0, 0)),
            pl.BlockSpec((1, block), columns),
            pl.BlockSpec((1, rows, block), lambda i: (0, 0, i)),
            pl.BlockSpec((count, rows, block), lambda i: (0, 0, i)),
            pl.BlockSpec((fresh_at, block), columns),
        ],
        out_specs=[
            pl.BlockSpec((rows, block), columns),
            pl.BlockSpec((copies, 128), lambda i: (0, 0)),
        ],
        out_shape=[
            jax.ShapeDtypeStruct((rows, width), f32),
            jax.ShapeDtypeStruct((copies, 128), f32),
        ],
        scratch_shapes=[pltpu.VMEM((fresh_at + padded(count + 1), block), f32)],
        cost_estimate=pl.CostEstimate(
            flops=20 * rows * width,
            bytes_accessed=hist_err.size * 2 + 14 * rows * width,
            transcendentals=0,
        ),
    )(ladder, source_terms, occ_energy, vir_energy, hist_amp, hist_err, stored)


def extrapolate(gathered, raw, hist_amp):
    count, rows, width = hist_amp.shape
    order = count + 1
    block = column_block(width)

    def solve(totals):
        lane = lax.broadcasted_iota(jnp.int32, totals.shape, 1)
        corr = {}
        for k in range(order):
            for m in range(k + 1):
                hit = lane == k * (k + 1) // 2 + m
                corr[k, m] = jnp.sum(jnp.where(hit, totals, 0.0), axis=1, keepdims=True)
        factor = {}
        for m in range(order):
            diag = corr[m, m]
            for j in range(m):
                diag = diag - factor[m, j] * factor[m, j]
            factor[m, m] = jnp.sqrt(diag)
            for k in range(m + 1, order):
                value = corr[k, m]
                for j in range(m):
                    value = value - factor[k, j] * factor[m, j]
                factor[k, m] = value / factor[m, m]
        forward = []
        for k in range(order):
            running = jnp.ones((1, 1), f32)
            for m in range(k):
                running = running - factor[k, m] * forward[m]
            forward.append(running / factor[k, k])
        backward = [None] * order
        for k in reversed(range(order)):
            running = forward[k]
            for m in range(k + 1, order):
                running = running - factor[m, k] * backward[m]
            backward[k] = running / factor[k, k]
        whole = backward[0]
        for k in range(1, order):
            whole = whole + backward[k]
        return [b / whole for b in backward]

    def kernel(sum_ref, raw_ref, amp_ref, out_ref, weight_ref):
        @pl.when(pl.program_id(0) == 0)
        def _():
            weights = solve(jnp.sum(sum_ref[...], axis=0, keepdims=True))
            for k in range(order):
                weight_ref[k : k + 1, :] = jnp.broadcast_to(weights[k], (1, 128))

        updated = weight_ref[count : count + 1, 0:1] * raw_ref[...]
        for k in range(count):
            updated = updated + weight_ref[k : k + 1, 0:1] * amp_ref[k].astype(f32)
        out_ref[...] = updated

    columns = lambda i: (0, i)
    return pl.pallas_call(
        kernel,
        grid=(width // block,),
        in_specs=[
            pl.BlockSpec(gathered.shape, lambda i: (0, 0)),
            pl.BlockSpec((rows, block), columns),
            pl.BlockSpec((count, rows, block), lambda i: (0, 0, i)),
        ],
        out_specs=pl.BlockSpec((rows, block), columns),
        out_shape=jax.ShapeDtypeStruct((rows, width), f32),
        scratch_shapes=[pltpu.VMEM((padded(order), 128), f32)],
    )(gathered, raw, hist_amp)


def cuts_of(rows):
    first = max(16, rows * 3 // 8 // 16 * 16)
    return [(at, min(first, rows - at)) for at in range(0, rows, first)]


def after(x, *earlier):
    return lax.optimization_barrier((x, *earlier))[0]


def make(mesh):
    row_n, col_n = mesh.shape["row"], mesh.shape["col"]
    total = row_n * col_n

    def send_col(x, m):
        return lax.ppermute(x, "col", [(i, i ^ m) for i in range(col_n)])

    def send_row(x, m):
        return lax.ppermute(x, "row", [(i, i ^ m) for i in range(row_n)])

    def on_device(
        integrals, lambda2, source_terms, hist_amp, hist_err, eps_occ, eps_vir, occ_pair, vir_pair
    ):
        rows, width = source_terms.shape
        depth = lambda2.shape[1]
        near = lambda2.shape[0] // rows
        r, c = lax.axis_index("row"), lax.axis_index("col")
        zi = r // near
        low = lax.rem(zi, 2) == lax.rem(c, 2)

        height = -(-rows // 16) * 16

        def multiply(piece):
            out = jnp.dot(
                piece.reshape(-1, depth), integrals, preferred_element_type=f32
            )
            return out.reshape(near, -1, width)

        def near_begin(part):
            bit = 1
            while True:
                halves = part.reshape(part.shape[0] // 2, 2, *part.shape[1:])
                mine = (r // bit) % 2 == 0
                send = jnp.where(mine, halves[:, 1], halves[:, 0]).astype(wire)
                keep = jnp.where(mine, halves[:, 0], halves[:, 1])
                taken = send_row(send, bit)
                if keep.shape[0] == 1:
                    return keep[0], taken[0], send
                part = keep + taken.astype(f32)
                bit *= 2

        def near_end(keep, taken):
            return keep + taken.astype(f32)

        def pair_begin(first, second):
            send = jnp.where(low, second, first).astype(wire)
            keep = jnp.where(low, first, second)
            return keep, send_row(send, near), send

        def far_begin(part, pair):
            kept = jnp.where(zi // 2 == (c // 2) ^ pair, part, 0.0)
            data = part.astype(wire)
            taken = []
            for d in range(1, col_n // 2):
                links = []
                for z in range(col_n):
                    for y in range(col_n):
                        if (z // 2) ^ (y // 2) ^ pair == d:
                            for x in range(near):
                                source = (z * near + x) * col_n + y
                                target = ((z ^ (2 * d)) * near + x) * col_n + y
                                links.append((source, target))
                taken.append(lax.ppermute(data, ("row", "col"), links))
            return kept, taken, data

        def far_end(kept, taken):
            for one in taken:
                kept = kept + one.astype(f32)
            return kept

        own = jnp.pad(
            lambda2.reshape(near, rows, depth), ((0, 0), (0, height - rows), (0, 0))
        )
        own = lax.optimization_barrier(own)
        cuts = cuts_of(height)
        stages = [(m, at, size) for m in range(2, col_n, 2) for at, size in cuts]
        last = len(stages) - 1
        far, nears, pairs, fars = {}, {}, {}, {}

        def start(n, *earlier):
            if n <= last:
                m, at, size = stages[n]
                far[n] = send_col(after(own[:, at : at + size], *earlier), m)

        start(0)
        start(1)
        sibling = send_col(own, 1)
        one = multiply(own)
        first = near_begin(one)
        two = multiply(after(sibling, first[2]))
        second = near_begin(two)
        stored = stored_products(after(hist_err, second[2]))
        nears[-1] = (first, second)
        token = stored

        def to_pair(n, token):
            (keep1, taken1, _), (keep2, taken2, _) = nears[n]
            taken1, taken2, _ = lax.optimization_barrier((taken1, taken2, token))
            pairs[n] = pair_begin(near_end(keep1, taken1), near_end(keep2, taken2))
            return pairs[n][2]

        def to_far(n, token):
            keep, taken, _ = pairs[n]
            taken = after(taken, token)
            m = stages[n][0] if n >= 0 else 0
            fars[n] = far_begin(near_end(keep, taken), m // 2)
            return fars[n][2]

        for n in range(last + 1):
            here = after(far[n], token)
            start(n + 2, here)
            swap = send_col(here, 1)
            one = multiply(here)
            two = multiply(after(swap, one))
            first, second = near_begin(one), near_begin(two)
            nears[n] = (first, second)
            token = second[2]
            token = to_pair(n - 1, token)
            if n >= 1:
                if n == 1:
                    token = to_far(-1, token)
                token = to_far(n - 1, token)
        token = to_pair(last, token)
        if last == 0:
            token = to_far(-1, token)
        token = to_far(last, token)

        ladder = far_end(*fars[-1][:2])
        for p in range(len(cuts), last + 2, len(cuts)):
            parts = [far_end(*fars[n][:2]) for n in range(p - len(cuts), p)]
            ladder = ladder + jnp.concatenate(parts, axis=0)

        occ_energy = jnp.broadcast_to(pair_energy(occ_pair, eps_occ)[:, None], (rows, 128))
        vir_energy = pair_energy(vir_pair, eps_vir)[None, :]
        raw, shares = new_products(
            ladder, source_terms, occ_energy, vir_energy, hist_amp, hist_err, stored, total
        )
        gathered = lax.all_to_all(shares, ("row", "col"), 0, 0, tiled=True)
        return extrapolate(gathered, raw, hist_amp)

    return on_device


def solution(mesh):
    placed = (
        P("row", "col"),
        P("col", "row"),
        P("row", "col"),
        P(None, "row", "col"),
        P(None, "row", "col"),
        P(),
        P(),
        P(None, "row"),
        P(None, "col"),
    )
    return jax.shard_map(
        make(mesh), mesh=mesh, in_specs=placed, out_specs=P("row", "col"), check_vma=False
    )
```

```python
import jax
import jax.numpy as jnp
from jax import lax
from jax.experimental import pallas as pl
from jax.experimental.pallas import tpu as pltpu
from jax.sharding import PartitionSpec as P

f32 = jnp.float32
wire = jnp.float16


def pair_energy(pairs, energies):
    levels = jnp.arange(energies.shape[0], dtype=jnp.int32)
    first = jnp.sum(jnp.where(pairs[0][:, None] == levels[None, :], energies[None, :], 0.0), axis=1)
    second = jnp.sum(
        jnp.where(pairs[1][:, None] == levels[None, :], energies[None, :], 0.0), axis=1
    )
    return first + second


def row_steps(rows, step, width, count, term):
    whole = rows // step

    def body(i, acc):
        parts = term(pl.ds(pl.multiple_of(i * step, step), step))
        return tuple(a + jnp.sum(p.reshape(step // 8, 8, width), axis=0) for a, p in zip(acc, parts))

    acc = tuple(jnp.zeros((8, width), f32) for _ in range(count))
    if whole:
        acc = lax.fori_loop(0, whole, body, acc, unroll=min(whole, 5))
    sums = [jnp.sum(a, axis=0, keepdims=True) for a in acc]
    if rows % step:
        parts = term(pl.ds(whole * step, rows % step))
        sums = [s + jnp.sum(p, axis=0, keepdims=True) for s, p in zip(sums, parts)]
    return sums


def column_block(width):
    return 256 if width % 256 == 0 else width


def padded(count):
    return -(-count // 8) * 8


def stored_products(hist_err):
    count, rows, width = hist_err.shape
    block = column_block(width)
    pairs = [(k, m) for k in range(count) for m in range(k + 1)]

    def kernel(err_ref, out_ref):
        def term(at):
            e = [err_ref[k, at, :].astype(f32) for k in range(count)]
            return [e[k] * e[m] for k, m in pairs]

        out_ref[...] = jnp.zeros_like(out_ref)
        for n, s in enumerate(row_steps(rows, 16, block, len(pairs), term)):
            out_ref[n : n + 1, :] = s

    return pl.pallas_call(
        kernel,
        grid=(width // block,),
        in_specs=[pl.BlockSpec((count, rows, block), lambda i: (0, 0, i))],
        out_specs=pl.BlockSpec((padded(len(pairs)), block), lambda i: (0, i)),
        out_shape=jax.ShapeDtypeStruct((padded(len(pairs)), width), f32),
        cost_estimate=pl.CostEstimate(
            flops=2 * len(pairs) * rows * width,
            bytes_accessed=hist_err.size * 2,
            transcendentals=0,
        ),
    )(hist_err)


def new_products(ladder, source_terms, occ_energy, vir_energy, hist_amp, hist_err, stored, copies):
    count, rows, width = hist_err.shape
    block = column_block(width)
    grid = width // block
    pairs = count * (count + 1) // 2
    fresh_at = stored.shape[0]

    def kernel(
        lad_ref, src_ref, occ_ref, vir_ref, amp_ref, err_ref, sto_ref, raw_ref, out_ref, sum_ref
    ):
        step = pl.program_id(0)

        @pl.when(step == 0)
        def _():
            sum_ref[...] = jnp.zeros_like(sum_ref)

        def term(at):
            den = occ_ref[at, 0:1] - vir_ref[...]
            raw = (src_ref[at, :] + lad_ref[at, :]) / den
            raw_ref[at, :] = raw
            new = raw - amp_ref[0, at, :].astype(f32)
            return [err_ref[k, at, :].astype(f32) * new for k in range(count)] + [new * new]

        sum_ref[0:fresh_at, :] += sto_ref[...]
        for n, s in enumerate(row_steps(rows, 16, block, count + 1, term)):
            sum_ref[fresh_at + n : fresh_at + n + 1, :] += s

        @pl.when(step == grid - 1)
        def _():
            column = jnp.sum(sum_ref[...], axis=1, keepdims=True)
            shape = (sum_ref.shape[0], 128)
            lane = lax.broadcasted_iota(jnp.int32, shape, 1)
            item = lax.broadcasted_iota(jnp.int32, shape, 0)
            place = jnp.where(item < fresh_at, item, item - fresh_at + pairs)
            used = (item < pairs) | (item >= fresh_at)
            spread = jnp.where((lane == place) & used, column, 0.0)
            out_ref[...] = jnp.broadcast_to(
                jnp.sum(spread, axis=0, keepdims=True), out_ref.shape
            )

    columns = lambda i: (0, i)
    return pl.pallas_call(
        kernel,
        grid=(grid,),
        in_specs=[
            pl.BlockSpec((ladder.shape[0], block), columns),
            pl.BlockSpec((rows, block), columns),
            pl.BlockSpec((rows, 128), lambda i: (0, 0)),
            pl.BlockSpec((1, block), columns),
            pl.BlockSpec((1, rows, block), lambda i: (0, 0, i)),
            pl.BlockSpec((count, rows, block), lambda i: (0, 0, i)),
            pl.BlockSpec((fresh_at, block), columns),
        ],
        out_specs=[
            pl.BlockSpec((rows, block), columns),
            pl.BlockSpec((copies, 128), lambda i: (0, 0)),
        ],
        out_shape=[
            jax.ShapeDtypeStruct((rows, width), f32),
            jax.ShapeDtypeStruct((copies, 128), f32),
        ],
        scratch_shapes=[pltpu.VMEM((fresh_at + padded(count + 1), block), f32)],
        cost_estimate=pl.CostEstimate(
            flops=20 * rows * width,
            bytes_accessed=hist_err.size * 2 + 14 * rows * width,
            transcendentals=0,
        ),
    )(ladder, source_terms, occ_energy, vir_energy, hist_amp, hist_err, stored)


def extrapolate(gathered, raw, hist_amp):
    count, rows, width = hist_amp.shape
    order = count + 1
    block = column_block(width)

    def solve(totals):
        lane = lax.broadcasted_iota(jnp.int32, totals.shape, 1)
        corr = {}
        for k in range(order):
            for m in range(k + 1):
                hit = lane == k * (k + 1) // 2 + m
                corr[k, m] = jnp.sum(jnp.where(hit, totals, 0.0), axis=1, keepdims=True)
        factor = {}
        for m in range(order):
            diag = corr[m, m]
            for j in range(m):
                diag = diag - factor[m, j] * factor[m, j]
            factor[m, m] = jnp.sqrt(diag)
            for k in range(m + 1, order):
                value = corr[k, m]
                for j in range(m):
                    value = value - factor[k, j] * factor[m, j]
                factor[k, m] = value / factor[m, m]
        forward = []
        for k in range(order):
            running = jnp.ones((1, 1), f32)
            for m in range(k):
                running = running - factor[k, m] * forward[m]
            forward.append(running / factor[k, k])
        backward = [None] * order
        for k in reversed(range(order)):
            running = forward[k]
            for m in range(k + 1, order):
                running = running - factor[m, k] * backward[m]
            backward[k] = running / factor[k, k]
        whole = backward[0]
        for k in range(1, order):
            whole = whole + backward[k]
        return [b / whole for b in backward]

    def kernel(sum_ref, raw_ref, amp_ref, out_ref, weight_ref):
        @pl.when(pl.program_id(0) == 0)
        def _():
            weights = solve(jnp.sum(sum_ref[...], axis=0, keepdims=True))
            for k in range(order):
                weight_ref[k : k + 1, :] = jnp.broadcast_to(weights[k], (1, 128))

        updated = weight_ref[count : count + 1, 0:1] * raw_ref[...]
        for k in range(count):
            updated = updated + weight_ref[k : k + 1, 0:1] * amp_ref[k].astype(f32)
        out_ref[...] = updated

    columns = lambda i: (0, i)
    return pl.pallas_call(
        kernel,
        grid=(width // block,),
        in_specs=[
            pl.BlockSpec(gathered.shape, lambda i: (0, 0)),
            pl.BlockSpec((rows, block), columns),
            pl.BlockSpec((count, rows, block), lambda i: (0, 0, i)),
        ],
        out_specs=pl.BlockSpec((rows, block), columns),
        out_shape=jax.ShapeDtypeStruct((rows, width), f32),
        scratch_shapes=[pltpu.VMEM((padded(order), 128), f32)],
    )(gathered, raw, hist_amp)


def cuts_of(rows):
    cuts, at = [], 0
    for part in (rows * 7 // 16, rows * 3 // 8):
        size = min(max(16, -(-part // 16) * 16), rows - at)
        if size:
            cuts.append((at, size))
        at += size
    if at < rows:
        cuts.append((at, rows - at))
    return cuts


def after(x, *earlier):
    return lax.optimization_barrier((x, *earlier))[0]


def make(mesh):
    row_n, col_n = mesh.shape["row"], mesh.shape["col"]
    total = row_n * col_n

    def send_col(x, m):
        return lax.ppermute(x, "col", [(i, i ^ m) for i in range(col_n)])

    def send_row(x, m):
        return lax.ppermute(x, "row", [(i, i ^ m) for i in range(row_n)])

    def on_device(
        integrals, lambda2, source_terms, hist_amp, hist_err, eps_occ, eps_vir, occ_pair, vir_pair
    ):
        rows, width = source_terms.shape
        depth = lambda2.shape[1]
        near = lambda2.shape[0] // rows
        r, c = lax.axis_index("row"), lax.axis_index("col")
        zi = r // near
        holder = lax.rem(zi, 2) == lax.rem(c, 2)
        height = -(-rows // 16) * 16

        def links_of(pair_of):
            links = []
            for z in range(col_n):
                for y in range(col_n):
                    z2 = pair_of(z, y)
                    if z2 is not None:
                        for x in range(near):
                            links.append(
                                ((z * near + x) * col_n + y, (z2 * near + x) * col_n + y)
                            )
            return links

        def multiply(piece, right):
            out = jnp.dot(
                piece.reshape(-1, depth), right, preferred_element_type=f32
            )
            return out.reshape(near, -1, width)

        def near_begin(part):
            bit = 1
            while True:
                count = part.shape[0]
                halves = part.reshape(count, part.shape[1] // 2, 2, *part.shape[2:])
                mine = (r // bit) % 2 == 0
                send = jnp.where(mine, halves[:, :, 1], halves[:, :, 0]).astype(wire)
                keep = jnp.where(mine, halves[:, :, 0], halves[:, :, 1])
                taken = send_row(send, bit)
                if keep.shape[1] == 1:
                    return keep[:, 0], taken[:, 0], send
                part = keep + taken.astype(f32)
                bit *= 2

        even_links = links_of(lambda z, y: z ^ 1 if (z ^ y) & 1 else None)

        def pair_begin(part):
            send = part.astype(wire)
            return part, lax.ppermute(send, ("row", "col"), even_links), send

        def far_begin(part, pair):
            kept = jnp.where(zi == c ^ (2 * pair), part, 0.0)
            data = part.astype(wire)
            taken = []
            for d in range(1, col_n // 2):
                links = links_of(
                    lambda z, y: z ^ (2 * d) if z ^ y ^ (2 * pair) == 2 * d else None
                )
                taken.append(lax.ppermute(data, ("row", "col"), links))
            return kept, taken, data

        def far_end(kept, taken):
            for one in taken:
                kept = kept + one.astype(f32)
            return kept

        def cut(at, size):
            parts = []
            for x in range(near):
                part = lambda2[x * rows + at : x * rows + min(at + size, rows)]
                parts.append(jnp.pad(part, ((0, size - part.shape[0]), (0, 0))))
            return jnp.stack(parts)

        cuts = cuts_of(height)
        stages = [(m, at, size) for m in range(2, col_n, 2) for at, size in cuts]
        far = {}

        def send_far(n, *earlier):
            if n < len(stages):
                m, at, size = stages[n]
                far[n] = send_col(lax.optimization_barrier((cut(at, size), *earlier))[0], m)
                return far[n]

        piece = lax.optimization_barrier(cut(*cuts[0]))
        far[0] = send_col(piece, stages[0][0])
        across = send_col(after(integrals, piece), 1)
        own = after(cut(0, height), piece)

        nears, pairs, fars = {}, {}, {}
        nears[0] = near_begin(multiply(own, integrals)[None])
        send_far(1, nears[0][2])
        stored = stored_products(after(hist_err, nears[0][2]))
        occ_energy = jnp.broadcast_to(pair_energy(occ_pair, eps_occ)[:, None], (rows, 128))
        vir_energy = pair_energy(vir_pair, eps_vir)[None, :]
        stored, occ_energy, vir_energy = lax.optimization_barrier((stored, occ_energy, vir_energy))
        across = after(across, stored)
        nears[1] = near_begin(multiply(own, across)[None])
        send_far(2, nears[1][2])
        last = len(stages) + 1

        def to_near(n, token):
            here = after(far[n - 2], token)
            send_far(n + 1, here)
            nears[n] = near_begin(
                jnp.stack([multiply(here, integrals), multiply(here, across)])
            )
            return nears[n][2]

        def to_pair(n, token):
            if 0 <= n <= last:
                keep, taken, _ = nears[n]
                pairs[n] = pair_begin(keep + after(taken, token).astype(f32))
                token = pairs[n][2]
            return token

        def to_far(n, token):
            if 0 <= n <= last:
                keep, taken, _ = pairs[n]
                kept = jnp.where(holder, keep, 0.0) + after(taken, token).astype(f32)
                fars[n] = far_begin(kept, stages[n - 2][0] // 2 if n >= 2 else 0)
                token = fars[n][2]
            return token

        token = nears[1][2]
        for n in range(2, last + 3):
            token = to_far(n - 3, token)
            token = to_pair(n - 2, token)
            if n <= last:
                token = to_near(n, token)
        token = to_far(last, token)

        first = far_end(*fars[0][:2])[0]
        second = far_end(*fars[1][:2])[0]
        done = []
        for q, (at, size) in enumerate(cuts):
            mine, other = first[at : at + size], second[at : at + size]
            for p in range(q + 2, last + 1, len(cuts)):
                total_rows = far_end(*fars[p][:2])
                mine, other = mine + total_rows[0], other + total_rows[1]
            done.append((mine, other))
        early = [other for _, other in done[:-1]]
        swapped = send_col(jnp.concatenate(early, axis=0), 1) if early else None
        swapped_last = send_col(done[-1][1], 1)
        taken = swapped_last if swapped is None else jnp.concatenate([swapped, swapped_last])
        ladder = jnp.concatenate([mine for mine, _ in done], axis=0) + taken

        raw, shares = new_products(
            ladder, source_terms, occ_energy, vir_energy, hist_amp, hist_err, stored, total
        )
        gathered = lax.all_to_all(shares, ("row", "col"), 0, 0, tiled=True)
        return extrapolate(gathered, raw, hist_amp)

    return on_device


def solution(mesh):
    placed = (
        P("row", "col"),
        P("col", "row"),
        P("row", "col"),
        P(None, "row", "col"),
        P(None, "row", "col"),
        P(),
        P(),
        P(None, "row"),
        P(None, "col"),
    )
    return jax.shard_map(
        make(mesh), mesh=mesh, in_specs=placed, out_specs=P("row", "col"), check_vma=False
    )
```

```python
import jax
import jax.numpy as jnp
from jax import lax
from jax.experimental import pallas as pl
from jax.experimental.pallas import tpu as pltpu
from jax.sharding import PartitionSpec as P

f32 = jnp.float32
small = pltpu.CompilerParams(vmem_limit_bytes=10 * 1024 * 1024)
wire = jnp.float16


def pair_energy(pairs, energies):
    levels = jnp.arange(energies.shape[0], dtype=jnp.int32)
    first = jnp.sum(jnp.where(pairs[0][:, None] == levels[None, :], energies[None, :], 0.0), axis=1)
    second = jnp.sum(
        jnp.where(pairs[1][:, None] == levels[None, :], energies[None, :], 0.0), axis=1
    )
    return first + second


def row_steps(rows, step, width, count, term):
    whole = rows // step

    def body(i, acc):
        parts = term(pl.ds(pl.multiple_of(i * step, step), step))
        return tuple(a + jnp.sum(p.reshape(step // 8, 8, width), axis=0) for a, p in zip(acc, parts))

    acc = tuple(jnp.zeros((8, width), f32) for _ in range(count))
    if whole:
        acc = lax.fori_loop(0, whole, body, acc, unroll=min(whole, 5))
    sums = [jnp.sum(a, axis=0, keepdims=True) for a in acc]
    if rows % step:
        parts = term(pl.ds(whole * step, rows % step))
        sums = [s + jnp.sum(p, axis=0, keepdims=True) for s, p in zip(sums, parts)]
    return sums


def column_block(width):
    return 256 if width % 256 == 0 else width


def padded(count):
    return -(-count // 8) * 8


def product_and_hold(left, right):
    rows, depth = left.shape
    width = right.shape[1]
    block = column_block(width)

    def kernel(left_ref, right_ref, out_ref, held_ref):
        at = pl.ds(pl.multiple_of(pl.program_id(0) * block, block), block)
        held_ref[:, at] = right_ref[...]
        out_ref[...] = jnp.dot(left_ref[...], right_ref[...], preferred_element_type=f32)

    return pl.pallas_call(
        kernel,
        grid=(width // block,),
        in_specs=[
            pl.BlockSpec((rows, depth), lambda i: (0, 0)),
            pl.BlockSpec((depth, block), lambda i: (0, i)),
        ],
        out_specs=[
            pl.BlockSpec((rows, block), lambda i: (0, i)),
            pl.BlockSpec(memory_space=pltpu.VMEM),
        ],
        out_shape=[
            jax.ShapeDtypeStruct((rows, width), f32),
            pltpu.VMEM((depth, width), right.dtype),
        ],
        compiler_params=small,
        cost_estimate=pl.CostEstimate(
            flops=2 * rows * depth * width,
            bytes_accessed=2 * depth * (rows + width),
            transcendentals=0,
        ),
    )(left, right)


def stored_products(hist_err):
    count, rows, width = hist_err.shape
    block = column_block(width)
    pairs = [(k, m) for k in range(count) for m in range(k + 1)]

    def kernel(err_ref, out_ref):
        def term(at):
            e = [err_ref[k, at, :].astype(f32) for k in range(count)]
            return [e[k] * e[m] for k, m in pairs]

        out_ref[...] = jnp.zeros_like(out_ref)
        for n, s in enumerate(row_steps(rows, 16, block, len(pairs), term)):
            out_ref[n : n + 1, :] = s

    return pl.pallas_call(
        kernel,
        compiler_params=small,
        grid=(width // block,),
        in_specs=[pl.BlockSpec((count, rows, block), lambda i: (0, 0, i))],
        out_specs=pl.BlockSpec((padded(len(pairs)), block), lambda i: (0, i)),
        out_shape=jax.ShapeDtypeStruct((padded(len(pairs)), width), f32),
        cost_estimate=pl.CostEstimate(
            flops=2 * len(pairs) * rows * width,
            bytes_accessed=hist_err.size * 2,
            transcendentals=0,
        ),
    )(hist_err)


def new_products(ladder, source_terms, occ_energy, vir_energy, hist_amp, hist_err, stored, copies):
    count, rows, width = hist_err.shape
    block = column_block(width)
    grid = width // block
    pairs = count * (count + 1) // 2
    fresh_at = stored.shape[0]

    def kernel(
        lad_ref, src_ref, occ_ref, vir_ref, amp_ref, err_ref, sto_ref, raw_ref, out_ref, sum_ref
    ):
        step = pl.program_id(0)

        @pl.when(step == 0)
        def _():
            sum_ref[...] = jnp.zeros_like(sum_ref)

        def term(at):
            den = occ_ref[at, 0:1] - vir_ref[...]
            raw = (src_ref[at, :] + lad_ref[at, :]) / den
            raw_ref[at, :] = raw
            new = raw - amp_ref[0, at, :].astype(f32)
            return [err_ref[k, at, :].astype(f32) * new for k in range(count)] + [new * new]

        sum_ref[0:fresh_at, :] += sto_ref[...]
        for n, s in enumerate(row_steps(rows, 16, block, count + 1, term)):
            sum_ref[fresh_at + n : fresh_at + n + 1, :] += s

        @pl.when(step == grid - 1)
        def _():
            column = jnp.sum(sum_ref[...], axis=1, keepdims=True)
            shape = (sum_ref.shape[0], 128)
            lane = lax.broadcasted_iota(jnp.int32, shape, 1)
            item = lax.broadcasted_iota(jnp.int32, shape, 0)
            place = jnp.where(item < fresh_at, item, item - fresh_at + pairs)
            used = (item < pairs) | (item >= fresh_at)
            spread = jnp.where((lane == place) & used, column, 0.0)
            out_ref[...] = jnp.broadcast_to(
                jnp.sum(spread, axis=0, keepdims=True), out_ref.shape
            )

    columns = lambda i: (0, i)
    return pl.pallas_call(
        kernel,
        compiler_params=small,
        grid=(grid,),
        in_specs=[
            pl.BlockSpec((ladder.shape[0], block), columns),
            pl.BlockSpec((rows, block), columns),
            pl.BlockSpec((rows, 128), lambda i: (0, 0)),
            pl.BlockSpec((1, block), columns),
            pl.BlockSpec((1, rows, block), lambda i: (0, 0, i)),
            pl.BlockSpec((count, rows, block), lambda i: (0, 0, i)),
            pl.BlockSpec((fresh_at, block), columns),
        ],
        out_specs=[
            pl.BlockSpec((rows, block), columns),
            pl.BlockSpec((copies, 128), lambda i: (0, 0)),
        ],
        out_shape=[
            jax.ShapeDtypeStruct((rows, width), f32),
            jax.ShapeDtypeStruct((copies, 128), f32),
        ],
        scratch_shapes=[pltpu.VMEM((fresh_at + padded(count + 1), block), f32)],
        cost_estimate=pl.CostEstimate(
            flops=20 * rows * width,
            bytes_accessed=hist_err.size * 2 + 14 * rows * width,
            transcendentals=0,
        ),
    )(ladder, source_terms, occ_energy, vir_energy, hist_amp, hist_err, stored)


def extrapolate(gathered, raw, hist_amp):
    count, rows, width = hist_amp.shape
    order = count + 1
    block = column_block(width)

    def solve(totals):
        lane = lax.broadcasted_iota(jnp.int32, totals.shape, 1)
        corr = {}
        for k in range(order):
            for m in range(k + 1):
                hit = lane == k * (k + 1) // 2 + m
                corr[k, m] = jnp.sum(jnp.where(hit, totals, 0.0), axis=1, keepdims=True)
        factor = {}
        for m in range(order):
            diag = corr[m, m]
            for j in range(m):
                diag = diag - factor[m, j] * factor[m, j]
            factor[m, m] = jnp.sqrt(diag)
            for k in range(m + 1, order):
                value = corr[k, m]
                for j in range(m):
                    value = value - factor[k, j] * factor[m, j]
                factor[k, m] = value / factor[m, m]
        forward = []
        for k in range(order):
            running = jnp.ones((1, 1), f32)
            for m in range(k):
                running = running - factor[k, m] * forward[m]
            forward.append(running / factor[k, k])
        backward = [None] * order
        for k in reversed(range(order)):
            running = forward[k]
            for m in range(k + 1, order):
                running = running - factor[m, k] * backward[m]
            backward[k] = running / factor[k, k]
        whole = backward[0]
        for k in range(1, order):
            whole = whole + backward[k]
        return [b / whole for b in backward]

    def kernel(sum_ref, raw_ref, amp_ref, out_ref, weight_ref):
        @pl.when(pl.program_id(0) == 0)
        def _():
            weights = solve(jnp.sum(sum_ref[...], axis=0, keepdims=True))
            for k in range(order):
                weight_ref[k : k + 1, :] = jnp.broadcast_to(weights[k], (1, 128))

        updated = weight_ref[count : count + 1, 0:1] * raw_ref[...]
        for k in range(count):
            updated = updated + weight_ref[k : k + 1, 0:1] * amp_ref[k].astype(f32)
        out_ref[...] = updated

    columns = lambda i: (0, i)
    return pl.pallas_call(
        kernel,
        compiler_params=small,
        grid=(width // block,),
        in_specs=[
            pl.BlockSpec(gathered.shape, lambda i: (0, 0)),
            pl.BlockSpec((rows, block), columns),
            pl.BlockSpec((count, rows, block), lambda i: (0, 0, i)),
        ],
        out_specs=pl.BlockSpec((rows, block), columns),
        out_shape=jax.ShapeDtypeStruct((rows, width), f32),
        scratch_shapes=[pltpu.VMEM((padded(order), 128), f32)],
    )(gathered, raw, hist_amp)


def cuts_of(rows):
    cuts, at = [], 0
    for part in (rows * 3 // 8, rows * 5 // 16):
        size = min(max(16, -(-part // 16) * 16), rows - at)
        if size:
            cuts.append((at, size))
        at += size
    if at < rows:
        cuts.append((at, rows - at))
    return cuts


def order_of(last):
    steps = ["p0", "n2", "p1", "f0"]
    for n in range(3, last + 1):
        if n > 3:
            steps.append(f"p{n - 1}")
        steps.append(f"n{n}")
        if n == 3:
            steps += ["p2", "s0"]
        else:
            steps.append(f"f{n - 2}")
    if last < 3:
        steps.append("s0")
    steps += [f"p{last}", "f1"]
    return steps + [f"f{n}" for n in range(max(2, last - 1), last + 1)]


def after(x, *earlier):
    return lax.optimization_barrier((x, *earlier))[0]


def make(mesh):
    row_n, col_n = mesh.shape["row"], mesh.shape["col"]
    total = row_n * col_n

    def send_col(x, m):
        return lax.ppermute(x, "col", [(i, i ^ m) for i in range(col_n)])

    def send_row(x, m):
        return lax.ppermute(x, "row", [(i, i ^ m) for i in range(row_n)])

    def on_device(
        integrals, lambda2, source_terms, hist_amp, hist_err, eps_occ, eps_vir, occ_pair, vir_pair
    ):
        rows, width = source_terms.shape
        depth = lambda2.shape[1]
        near = lambda2.shape[0] // rows
        r, c = lax.axis_index("row"), lax.axis_index("col")
        zi = r // near
        holder = lax.rem(zi, 2) == lax.rem(c, 2)
        height = -(-rows // 16) * 16

        def links_of(pair_of):
            links = []
            for z in range(col_n):
                for y in range(col_n):
                    z2 = pair_of(z, y)
                    if z2 is not None:
                        for x in range(near):
                            links.append(
                                ((z * near + x) * col_n + y, (z2 * near + x) * col_n + y)
                            )
            return links

        def multiply(piece, right):
            out = jnp.dot(
                piece.reshape(-1, depth), right, preferred_element_type=f32
            )
            return out.reshape(near, -1, width)

        def near_begin(part):
            bit = 1
            while True:
                count = part.shape[0]
                halves = part.reshape(count, part.shape[1] // 2, 2, *part.shape[2:])
                mine = (r // bit) % 2 == 0
                send = jnp.where(mine, halves[:, :, 1], halves[:, :, 0]).astype(wire)
                keep = jnp.where(mine, halves[:, :, 0], halves[:, :, 1])
                taken = send_row(send, bit)
                if keep.shape[1] == 1:
                    return keep[:, 0], taken[:, 0], send
                part = keep + taken.astype(f32)
                bit *= 2

        even_links = links_of(lambda z, y: z ^ 1 if (z ^ y) & 1 else None)

        def pair_begin(part):
            send = part.astype(wire)
            return part, lax.ppermute(send, ("row", "col"), even_links), send

        def far_begin(part, pair):
            kept = jnp.where(zi == c ^ (2 * pair), part, 0.0)
            data = part.astype(wire)
            taken = []
            for d in range(1, col_n // 2):
                links = links_of(
                    lambda z, y: z ^ (2 * d) if z ^ y ^ (2 * pair) == 2 * d else None
                )
                taken.append(lax.ppermute(data, ("row", "col"), links))
            return kept, taken, data

        def far_end(kept, taken):
            for one in taken:
                kept = kept + one.astype(f32)
            return kept

        def cut(at, size):
            parts = []
            for x in range(near):
                part = lambda2[x * rows + at : x * rows + min(at + size, rows)]
                parts.append(jnp.pad(part, ((0, size - part.shape[0]), (0, 0))))
            return jnp.stack(parts)

        cuts = cuts_of(height)
        stages = [(m, at, size) for m in range(2, col_n, 2) for at, size in cuts]
        far = {}

        def send_far(n, *earlier):
            if n < len(stages):
                m, at, size = stages[n]
                far[n] = send_col(lax.optimization_barrier((cut(at, size), *earlier))[0], m)
                return far[n]

        piece = lax.optimization_barrier(cut(*cuts[0]))
        far[0] = send_col(piece, stages[0][0])
        across = send_col(after(integrals, piece), 1)
        own = after(cut(0, height), piece)

        nears, pairs, fars = {}, {}, {}
        nears[0] = near_begin(multiply(own, integrals)[None])
        send_far(1, nears[0][2])
        across = after(across, nears[0][2])
        beside, across = product_and_hold(own.reshape(-1, depth), across)
        nears[1] = near_begin(beside.reshape(1, near, -1, width))
        send_far(2, nears[1][2])
        last = len(stages) + 1

        def to_near(n, token):
            here = after(far[n - 2], token)
            send_far(n + 1, here)
            nears[n] = near_begin(
                jnp.stack([multiply(here, integrals), multiply(here, across)])
            )
            return nears[n][2]

        def to_pair(n, token):
            keep, taken, _ = nears[n]
            pairs[n] = pair_begin(keep + after(taken, token).astype(f32))
            return pairs[n][2]

        def to_far(n, token):
            keep, taken, _ = pairs[n]
            kept = jnp.where(holder, keep, 0.0) + after(taken, token).astype(f32)
            fars[n] = far_begin(kept, stages[n - 2][0] // 2 if n >= 2 else 0)
            return fars[n][2]

        def reduce_stored(token):
            out = stored_products(after(hist_err, token))
            occ = jnp.broadcast_to(pair_energy(occ_pair, eps_occ)[:, None], (rows, 128))
            vir = pair_energy(vir_pair, eps_vir)[None, :]
            return lax.optimization_barrier((out, occ, vir))

        token = nears[1][2]
        for step in order_of(last):
            kind, n = step[0], int(step[1:])
            if kind == "s":
                stored, occ_energy, vir_energy = reduce_stored(token)
                token = stored
            else:
                token = {"n": to_near, "p": to_pair, "f": to_far}[kind](n, token)

        first = far_end(*fars[0][:2])[0]
        second = far_end(*fars[1][:2])[0]
        done = []
        for q, (at, size) in enumerate(cuts):
            mine, other = first[at : at + size], second[at : at + size]
            for p in range(q + 2, last + 1, len(cuts)):
                total_rows = far_end(*fars[p][:2])
                mine, other = mine + total_rows[0], other + total_rows[1]
            done.append((mine, other))
        early = [other for _, other in done[:-1]]
        swapped = send_col(jnp.concatenate(early, axis=0), 1) if early else None
        swapped_last = send_col(done[-1][1], 1)
        taken = swapped_last if swapped is None else jnp.concatenate([swapped, swapped_last])
        ladder = jnp.concatenate([mine for mine, _ in done], axis=0) + taken

        raw, shares = new_products(
            ladder, source_terms, occ_energy, vir_energy, hist_amp, hist_err, stored, total
        )
        gathered = lax.all_to_all(shares, ("row", "col"), 0, 0, tiled=True)
        return extrapolate(gathered, raw, hist_amp)

    return on_device


def solution(mesh):
    placed = (
        P("row", "col"),
        P("col", "row"),
        P("row", "col"),
        P(None, "row", "col"),
        P(None, "row", "col"),
        P(),
        P(),
        P(None, "row"),
        P(None, "col"),
    )
    return jax.shard_map(
        make(mesh), mesh=mesh, in_specs=placed, out_specs=P("row", "col"), check_vma=False
    )
```

```python
import jax
import jax.numpy as jnp
from jax import lax
from jax.experimental import pallas as pl
from jax.experimental.pallas import tpu as pltpu
from jax.sharding import PartitionSpec as P

f32 = jnp.float32
small = pltpu.CompilerParams(vmem_limit_bytes=10 * 1024 * 1024)
wire = jnp.float16


def pair_energy(pairs, energies):
    levels = jnp.arange(energies.shape[0], dtype=jnp.int32)
    first = jnp.sum(jnp.where(pairs[0][:, None] == levels[None, :], energies[None, :], 0.0), axis=1)
    second = jnp.sum(
        jnp.where(pairs[1][:, None] == levels[None, :], energies[None, :], 0.0), axis=1
    )
    return first + second


def row_steps(rows, step, width, count, term):
    whole = rows // step

    def body(i, acc):
        parts = term(pl.ds(pl.multiple_of(i * step, step), step))
        return tuple(a + jnp.sum(p.reshape(step // 8, 8, width), axis=0) for a, p in zip(acc, parts))

    acc = tuple(jnp.zeros((8, width), f32) for _ in range(count))
    if whole:
        acc = lax.fori_loop(0, whole, body, acc, unroll=min(whole, 5))
    sums = [jnp.sum(a, axis=0, keepdims=True) for a in acc]
    if rows % step:
        parts = term(pl.ds(whole * step, rows % step))
        sums = [s + jnp.sum(p, axis=0, keepdims=True) for s, p in zip(sums, parts)]
    return sums


def column_block(width):
    return 256 if width % 256 == 0 else width


def padded(count):
    return -(-count // 8) * 8


def product_and_hold(left, right):
    rows, depth = left.shape
    width = right.shape[1]
    block = column_block(width)

    def kernel(left_ref, right_ref, out_ref, held_ref):
        at = pl.ds(pl.multiple_of(pl.program_id(0) * block, block), block)
        held_ref[:, at] = right_ref[...]
        out_ref[...] = jnp.dot(left_ref[...], right_ref[...], preferred_element_type=f32)

    return pl.pallas_call(
        kernel,
        grid=(width // block,),
        in_specs=[
            pl.BlockSpec((rows, depth), lambda i: (0, 0)),
            pl.BlockSpec((depth, block), lambda i: (0, i)),
        ],
        out_specs=[
            pl.BlockSpec((rows, block), lambda i: (0, i)),
            pl.BlockSpec(memory_space=pltpu.VMEM),
        ],
        out_shape=[
            jax.ShapeDtypeStruct((rows, width), f32),
            pltpu.VMEM((depth, width), right.dtype),
        ],
        compiler_params=small,
        cost_estimate=pl.CostEstimate(
            flops=2 * rows * depth * width,
            bytes_accessed=2 * depth * (rows + width),
            transcendentals=0,
        ),
    )(left, right)


def stored_products(hist_err):
    count, rows, width = hist_err.shape
    block = column_block(width)
    pairs = [(k, m) for k in range(count) for m in range(k + 1)]

    def kernel(err_ref, out_ref):
        def term(at):
            e = [err_ref[k, at, :].astype(f32) for k in range(count)]
            return [e[k] * e[m] for k, m in pairs]

        out_ref[...] = jnp.zeros_like(out_ref)
        for n, s in enumerate(row_steps(rows, 16, block, len(pairs), term)):
            out_ref[n : n + 1, :] = s

    return pl.pallas_call(
        kernel,
        compiler_params=small,
        grid=(width // block,),
        in_specs=[pl.BlockSpec((count, rows, block), lambda i: (0, 0, i))],
        out_specs=pl.BlockSpec((padded(len(pairs)), block), lambda i: (0, i)),
        out_shape=jax.ShapeDtypeStruct((padded(len(pairs)), width), f32),
        cost_estimate=pl.CostEstimate(
            flops=2 * len(pairs) * rows * width,
            bytes_accessed=hist_err.size * 2,
            transcendentals=0,
        ),
    )(hist_err)


def new_products(ladder, source_terms, occ_energy, vir_energy, hist_amp, hist_err, stored, copies):
    count, rows, width = hist_err.shape
    block = column_block(width)
    grid = width // block
    pairs = count * (count + 1) // 2
    fresh_at = stored.shape[0]

    def kernel(
        lad_ref, src_ref, occ_ref, vir_ref, amp_ref, err_ref, sto_ref, raw_ref, out_ref, sum_ref
    ):
        step = pl.program_id(0)

        @pl.when(step == 0)
        def _():
            sum_ref[...] = jnp.zeros_like(sum_ref)

        def term(at):
            den = occ_ref[at, 0:1] - vir_ref[...]
            raw = (src_ref[at, :] + lad_ref[at, :]) / den
            raw_ref[at, :] = raw
            new = raw - amp_ref[0, at, :].astype(f32)
            return [err_ref[k, at, :].astype(f32) * new for k in range(count)] + [new * new]

        sum_ref[0:fresh_at, :] += sto_ref[...]
        for n, s in enumerate(row_steps(rows, 16, block, count + 1, term)):
            sum_ref[fresh_at + n : fresh_at + n + 1, :] += s

        @pl.when(step == grid - 1)
        def _():
            column = jnp.sum(sum_ref[...], axis=1, keepdims=True)
            shape = (sum_ref.shape[0], 128)
            lane = lax.broadcasted_iota(jnp.int32, shape, 1)
            item = lax.broadcasted_iota(jnp.int32, shape, 0)
            place = jnp.where(item < fresh_at, item, item - fresh_at + pairs)
            used = (item < pairs) | (item >= fresh_at)
            spread = jnp.where((lane == place) & used, column, 0.0)
            out_ref[...] = jnp.broadcast_to(
                jnp.sum(spread, axis=0, keepdims=True), out_ref.shape
            )

    columns = lambda i: (0, i)
    return pl.pallas_call(
        kernel,
        compiler_params=small,
        grid=(grid,),
        in_specs=[
            pl.BlockSpec((ladder.shape[0], block), columns),
            pl.BlockSpec((rows, block), columns),
            pl.BlockSpec((rows, 128), lambda i: (0, 0)),
            pl.BlockSpec((1, block), columns),
            pl.BlockSpec((1, rows, block), lambda i: (0, 0, i)),
            pl.BlockSpec((count, rows, block), lambda i: (0, 0, i)),
            pl.BlockSpec((fresh_at, block), columns),
        ],
        out_specs=[
            pl.BlockSpec((rows, block), columns),
            pl.BlockSpec((copies, 128), lambda i: (0, 0)),
        ],
        out_shape=[
            jax.ShapeDtypeStruct((rows, width), f32),
            jax.ShapeDtypeStruct((copies, 128), f32),
        ],
        scratch_shapes=[pltpu.VMEM((fresh_at + padded(count + 1), block), f32)],
        cost_estimate=pl.CostEstimate(
            flops=20 * rows * width,
            bytes_accessed=hist_err.size * 2 + 14 * rows * width,
            transcendentals=0,
        ),
    )(ladder, source_terms, occ_energy, vir_energy, hist_amp, hist_err, stored)


def extrapolate(gathered, raw, hist_amp):
    count, rows, width = hist_amp.shape
    order = count + 1
    block = column_block(width)

    def solve(totals):
        lane = lax.broadcasted_iota(jnp.int32, totals.shape, 1)
        corr = {}
        for k in range(order):
            for m in range(k + 1):
                hit = lane == k * (k + 1) // 2 + m
                corr[k, m] = jnp.sum(jnp.where(hit, totals, 0.0), axis=1, keepdims=True)
        factor = {}
        for m in range(order):
            diag = corr[m, m]
            for j in range(m):
                diag = diag - factor[m, j] * factor[m, j]
            factor[m, m] = jnp.sqrt(diag)
            for k in range(m + 1, order):
                value = corr[k, m]
                for j in range(m):
                    value = value - factor[k, j] * factor[m, j]
                factor[k, m] = value / factor[m, m]
        forward = []
        for k in range(order):
            running = jnp.ones((1, 1), f32)
            for m in range(k):
                running = running - factor[k, m] * forward[m]
            forward.append(running / factor[k, k])
        backward = [None] * order
        for k in reversed(range(order)):
            running = forward[k]
            for m in range(k + 1, order):
                running = running - factor[m, k] * backward[m]
            backward[k] = running / factor[k, k]
        whole = backward[0]
        for k in range(1, order):
            whole = whole + backward[k]
        return [b / whole for b in backward]

    def kernel(sum_ref, raw_ref, amp_ref, out_ref, weight_ref):
        @pl.when(pl.program_id(0) == 0)
        def _():
            weights = solve(jnp.sum(sum_ref[...], axis=0, keepdims=True))
            for k in range(order):
                weight_ref[k : k + 1, :] = jnp.broadcast_to(weights[k], (1, 128))

        updated = weight_ref[count : count + 1, 0:1] * raw_ref[...]
        for k in range(count):
            updated = updated + weight_ref[k : k + 1, 0:1] * amp_ref[k].astype(f32)
        out_ref[...] = updated

    columns = lambda i: (0, i)
    return pl.pallas_call(
        kernel,
        compiler_params=small,
        grid=(width // block,),
        in_specs=[
            pl.BlockSpec(gathered.shape, lambda i: (0, 0)),
            pl.BlockSpec((rows, block), columns),
            pl.BlockSpec((count, rows, block), lambda i: (0, 0, i)),
        ],
        out_specs=pl.BlockSpec((rows, block), columns),
        out_shape=jax.ShapeDtypeStruct((rows, width), f32),
        scratch_shapes=[pltpu.VMEM((padded(order), 128), f32)],
    )(gathered, raw, hist_amp)


def cuts_of(rows):
    cuts, at = [], 0
    for part in (rows * 3 // 8, rows * 5 // 16):
        size = min(max(16, -(-part // 16) * 16), rows - at)
        if size:
            cuts.append((at, size))
        at += size
    if at < rows:
        cuts.append((at, rows - at))
    return cuts


def order_of(last):
    steps = ["p0", "n2", "p1", "f0"]
    for n in range(3, last + 1):
        steps += [f"n{n}", f"p{n - 1}"]
        steps.append("s0" if n == 3 else f"f{n - 2}")
    if last < 3:
        steps.append("s0")
    steps += [f"p{last}", "f1"]
    return steps + [f"f{n}" for n in range(max(2, last - 1), last + 1)]


def after(x, *earlier):
    return lax.optimization_barrier((x, *earlier))[0]


def make(mesh):
    row_n, col_n = mesh.shape["row"], mesh.shape["col"]
    total = row_n * col_n

    def send_col(x, m):
        return lax.ppermute(x, "col", [(i, i ^ m) for i in range(col_n)])

    def send_row(x, m):
        return lax.ppermute(x, "row", [(i, i ^ m) for i in range(row_n)])

    def on_device(
        integrals, lambda2, source_terms, hist_amp, hist_err, eps_occ, eps_vir, occ_pair, vir_pair
    ):
        rows, width = source_terms.shape
        depth = lambda2.shape[1]
        near = lambda2.shape[0] // rows
        r, c = lax.axis_index("row"), lax.axis_index("col")
        zi = r // near
        holder = lax.rem(zi, 2) == lax.rem(c, 2)
        height = -(-rows // 16) * 16

        def links_of(pair_of):
            links = []
            for z in range(col_n):
                for y in range(col_n):
                    z2 = pair_of(z, y)
                    if z2 is not None:
                        for x in range(near):
                            links.append(
                                ((z * near + x) * col_n + y, (z2 * near + x) * col_n + y)
                            )
            return links

        def multiply(piece, right):
            out = jnp.dot(
                piece.reshape(-1, depth), right, preferred_element_type=f32
            )
            return out.reshape(near, -1, width)

        def near_begin(part):
            bit = 1
            while True:
                count = part.shape[0]
                halves = part.reshape(count, part.shape[1] // 2, 2, *part.shape[2:])
                mine = (r // bit) % 2 == 0
                send = jnp.where(mine, halves[:, :, 1], halves[:, :, 0]).astype(wire)
                keep = jnp.where(mine, halves[:, :, 0], halves[:, :, 1])
                taken = send_row(send, bit)
                if keep.shape[1] == 1:
                    return keep[:, 0], taken[:, 0], send
                part = keep + taken.astype(f32)
                bit *= 2

        even_links = links_of(lambda z, y: z ^ 1 if (z ^ y) & 1 else None)

        def pair_begin(part):
            send = part.astype(wire)
            return part, lax.ppermute(send, ("row", "col"), even_links), send

        def far_begin(part, pair):
            kept = jnp.where(zi == c ^ (2 * pair), part, 0.0)
            data = part.astype(wire)
            taken = []
            for d in range(1, col_n // 2):
                links = links_of(
                    lambda z, y: z ^ (2 * d) if z ^ y ^ (2 * pair) == 2 * d else None
                )
                taken.append(lax.ppermute(data, ("row", "col"), links))
            return kept, taken, data

        def far_end(kept, taken):
            for one in taken:
                kept = kept + one.astype(f32)
            return kept

        def cut(at, size):
            parts = []
            for x in range(near):
                part = lambda2[x * rows + at : x * rows + min(at + size, rows)]
                parts.append(jnp.pad(part, ((0, size - part.shape[0]), (0, 0))))
            return jnp.stack(parts)

        cuts = cuts_of(height)
        stages = [(m, at, size) for m in range(2, col_n, 2) for at, size in cuts]
        far = {}

        def send_far(n, *earlier):
            if n < len(stages):
                m, at, size = stages[n]
                far[n] = send_col(lax.optimization_barrier((cut(at, size), *earlier))[0], m)
                return far[n]

        piece = lax.optimization_barrier(cut(*cuts[0]))
        far[0] = send_col(piece, stages[0][0])
        across = send_col(after(integrals, piece), 1)
        own = after(cut(0, height), piece)

        nears, pairs, fars = {}, {}, {}
        nears[0] = near_begin(multiply(own, integrals)[None])
        send_far(1, nears[0][2])
        across = after(across, nears[0][2])
        beside, across = product_and_hold(own.reshape(-1, depth), across)
        nears[1] = near_begin(beside.reshape(1, near, -1, width))
        send_far(2, nears[1][2])
        last = len(stages) + 1

        def to_near(n, token):
            here = after(far[n - 2], token)
            send_far(n + 1, here)
            nears[n] = near_begin(
                jnp.stack([multiply(here, integrals), multiply(here, across)])
            )
            return nears[n][2]

        def to_pair(n, token):
            keep, taken, _ = nears[n]
            pairs[n] = pair_begin(keep + after(taken, token).astype(f32))
            return pairs[n][2]

        def to_far(n, token):
            keep, taken, _ = pairs[n]
            kept = jnp.where(holder, keep, 0.0) + after(taken, token).astype(f32)
            fars[n] = far_begin(kept, stages[n - 2][0] // 2 if n >= 2 else 0)
            return fars[n][2]

        def reduce_stored(token):
            out = stored_products(after(hist_err, token))
            occ = jnp.broadcast_to(pair_energy(occ_pair, eps_occ)[:, None], (rows, 128))
            vir = pair_energy(vir_pair, eps_vir)[None, :]
            return lax.optimization_barrier((out, occ, vir))

        token = nears[1][2]
        for step in order_of(last):
            kind, n = step[0], int(step[1:])
            if kind == "s":
                stored, occ_energy, vir_energy = reduce_stored(token)
                token = stored
            else:
                token = {"n": to_near, "p": to_pair, "f": to_far}[kind](n, token)

        first = far_end(*fars[0][:2])[0]
        second = far_end(*fars[1][:2])[0]
        done = []
        for q, (at, size) in enumerate(cuts):
            mine, other = first[at : at + size], second[at : at + size]
            for p in range(q + 2, last + 1, len(cuts)):
                total_rows = far_end(*fars[p][:2])
                mine, other = mine + total_rows[0], other + total_rows[1]
            done.append((mine, other))
        early = [other for _, other in done[:-1]]
        swapped = send_col(jnp.concatenate(early, axis=0), 1) if early else None
        swapped_last = send_col(done[-1][1], 1)
        taken = swapped_last if swapped is None else jnp.concatenate([swapped, swapped_last])
        ladder = jnp.concatenate([mine for mine, _ in done], axis=0) + taken

        raw, shares = new_products(
            ladder, source_terms, occ_energy, vir_energy, hist_amp, hist_err, stored, total
        )
        gathered = lax.all_to_all(shares, ("row", "col"), 0, 0, tiled=True)
        return extrapolate(gathered, raw, hist_amp)

    return on_device


def solution(mesh):
    placed = (
        P("row", "col"),
        P("col", "row"),
        P("row", "col"),
        P(None, "row", "col"),
        P(None, "row", "col"),
        P(),
        P(),
        P(None, "row"),
        P(None, "col"),
    )
    return jax.shard_map(
        make(mesh), mesh=mesh, in_specs=placed, out_specs=P("row", "col"), check_vma=False
    )
```

```python
import jax
import jax.numpy as jnp
from jax import lax
from jax.experimental import pallas as pl
from jax.experimental.pallas import tpu as pltpu
from jax.sharding import PartitionSpec as P

f32 = jnp.float32
small = pltpu.CompilerParams(vmem_limit_bytes=10 * 1024 * 1024)
wire = jnp.float16


def pair_energy(pairs, energies):
    levels = jnp.arange(energies.shape[0], dtype=jnp.int32)
    first = jnp.sum(jnp.where(pairs[0][:, None] == levels[None, :], energies[None, :], 0.0), axis=1)
    second = jnp.sum(
        jnp.where(pairs[1][:, None] == levels[None, :], energies[None, :], 0.0), axis=1
    )
    return first + second


def row_steps(rows, step, width, count, term):
    whole = rows // step

    def body(i, acc):
        parts = term(pl.ds(pl.multiple_of(i * step, step), step))
        return tuple(a + jnp.sum(p.reshape(step // 8, 8, width), axis=0) for a, p in zip(acc, parts))

    acc = tuple(jnp.zeros((8, width), f32) for _ in range(count))
    if whole:
        acc = lax.fori_loop(0, whole, body, acc, unroll=min(whole, 5))
    sums = [jnp.sum(a, axis=0, keepdims=True) for a in acc]
    if rows % step:
        parts = term(pl.ds(whole * step, rows % step))
        sums = [s + jnp.sum(p, axis=0, keepdims=True) for s, p in zip(sums, parts)]
    return sums


def column_block(width):
    return 256 if width % 256 == 0 else width


def padded(count):
    return -(-count // 8) * 8


def product_and_hold(left, right):
    rows, depth = left.shape
    width = right.shape[1]
    block = column_block(width)

    def kernel(left_ref, right_ref, out_ref, held_ref):
        at = pl.ds(pl.multiple_of(pl.program_id(0) * block, block), block)
        held_ref[:, at] = right_ref[...]
        out_ref[...] = jnp.dot(left_ref[...], right_ref[...], preferred_element_type=f32)

    return pl.pallas_call(
        kernel,
        grid=(width // block,),
        in_specs=[
            pl.BlockSpec((rows, depth), lambda i: (0, 0)),
            pl.BlockSpec((depth, block), lambda i: (0, i)),
        ],
        out_specs=[
            pl.BlockSpec((rows, block), lambda i: (0, i)),
            pl.BlockSpec(memory_space=pltpu.VMEM),
        ],
        out_shape=[
            jax.ShapeDtypeStruct((rows, width), f32),
            pltpu.VMEM((depth, width), right.dtype),
        ],
        compiler_params=small,
        cost_estimate=pl.CostEstimate(
            flops=2 * rows * depth * width,
            bytes_accessed=2 * depth * (rows + width),
            transcendentals=0,
        ),
    )(left, right)


def stored_products(hist_err):
    count, rows, width = hist_err.shape
    block = column_block(width)
    pairs = [(k, m) for k in range(count) for m in range(k + 1)]

    def kernel(err_ref, out_ref):
        def term(at):
            e = [err_ref[k, at, :].astype(f32) for k in range(count)]
            return [e[k] * e[m] for k, m in pairs]

        out_ref[...] = jnp.zeros_like(out_ref)
        for n, s in enumerate(row_steps(rows, 16, block, len(pairs), term)):
            out_ref[n : n + 1, :] = s

    return pl.pallas_call(
        kernel,
        compiler_params=small,
        grid=(width // block,),
        in_specs=[pl.BlockSpec((count, rows, block), lambda i: (0, 0, i))],
        out_specs=pl.BlockSpec((padded(len(pairs)), block), lambda i: (0, i)),
        out_shape=jax.ShapeDtypeStruct((padded(len(pairs)), width), f32),
        cost_estimate=pl.CostEstimate(
            flops=2 * len(pairs) * rows * width,
            bytes_accessed=hist_err.size * 2,
            transcendentals=0,
        ),
    )(hist_err)


def new_products(ladder, source_terms, occ_energy, vir_energy, hist_amp, hist_err, stored, copies):
    count, rows, width = hist_err.shape
    block = column_block(width)
    grid = width // block
    pairs = count * (count + 1) // 2
    fresh_at = stored.shape[0]

    def kernel(
        lad_ref, src_ref, occ_ref, vir_ref, amp_ref, err_ref, sto_ref, raw_ref, out_ref, sum_ref
    ):
        step = pl.program_id(0)

        @pl.when(step == 0)
        def _():
            sum_ref[...] = jnp.zeros_like(sum_ref)

        def term(at):
            den = occ_ref[at, 0:1] - vir_ref[...]
            raw = (src_ref[at, :] + lad_ref[at, :]) / den
            raw_ref[at, :] = raw
            new = raw - amp_ref[0, at, :].astype(f32)
            return [err_ref[k, at, :].astype(f32) * new for k in range(count)] + [new * new]

        sum_ref[0:fresh_at, :] += sto_ref[...]
        for n, s in enumerate(row_steps(rows, 16, block, count + 1, term)):
            sum_ref[fresh_at + n : fresh_at + n + 1, :] += s

        @pl.when(step == grid - 1)
        def _():
            column = jnp.sum(sum_ref[...], axis=1, keepdims=True)
            shape = (sum_ref.shape[0], 128)
            lane = lax.broadcasted_iota(jnp.int32, shape, 1)
            item = lax.broadcasted_iota(jnp.int32, shape, 0)
            place = jnp.where(item < fresh_at, item, item - fresh_at + pairs)
            used = (item < pairs) | (item >= fresh_at)
            spread = jnp.where((lane == place) & used, column, 0.0)
            out_ref[...] = jnp.broadcast_to(
                jnp.sum(spread, axis=0, keepdims=True), out_ref.shape
            )

    columns = lambda i: (0, i)
    return pl.pallas_call(
        kernel,
        compiler_params=small,
        grid=(grid,),
        in_specs=[
            pl.BlockSpec((ladder.shape[0], block), columns),
            pl.BlockSpec((rows, block), columns),
            pl.BlockSpec((rows, 128), lambda i: (0, 0)),
            pl.BlockSpec((1, block), columns),
            pl.BlockSpec((1, rows, block), lambda i: (0, 0, i)),
            pl.BlockSpec((count, rows, block), lambda i: (0, 0, i)),
            pl.BlockSpec((fresh_at, block), columns),
        ],
        out_specs=[
            pl.BlockSpec((rows, block), columns),
            pl.BlockSpec((copies, 128), lambda i: (0, 0)),
        ],
        out_shape=[
            jax.ShapeDtypeStruct((rows, width), f32),
            jax.ShapeDtypeStruct((copies, 128), f32),
        ],
        scratch_shapes=[pltpu.VMEM((fresh_at + padded(count + 1), block), f32)],
        cost_estimate=pl.CostEstimate(
            flops=20 * rows * width,
            bytes_accessed=hist_err.size * 2 + 14 * rows * width,
            transcendentals=0,
        ),
    )(ladder, source_terms, occ_energy, vir_energy, hist_amp, hist_err, stored)


def extrapolate(gathered, raw, hist_amp):
    count, rows, width = hist_amp.shape
    order = count + 1
    block = column_block(width)

    def solve(totals):
        lane = lax.broadcasted_iota(jnp.int32, totals.shape, 1)
        corr = {}
        for k in range(order):
            for m in range(k + 1):
                hit = lane == k * (k + 1) // 2 + m
                corr[k, m] = jnp.sum(jnp.where(hit, totals, 0.0), axis=1, keepdims=True)
        factor = {}
        for m in range(order):
            diag = corr[m, m]
            for j in range(m):
                diag = diag - factor[m, j] * factor[m, j]
            factor[m, m] = jnp.sqrt(diag)
            for k in range(m + 1, order):
                value = corr[k, m]
                for j in range(m):
                    value = value - factor[k, j] * factor[m, j]
                factor[k, m] = value / factor[m, m]
        forward = []
        for k in range(order):
            running = jnp.ones((1, 1), f32)
            for m in range(k):
                running = running - factor[k, m] * forward[m]
            forward.append(running / factor[k, k])
        backward = [None] * order
        for k in reversed(range(order)):
            running = forward[k]
            for m in range(k + 1, order):
                running = running - factor[m, k] * backward[m]
            backward[k] = running / factor[k, k]
        whole = backward[0]
        for k in range(1, order):
            whole = whole + backward[k]
        return [b / whole for b in backward]

    def kernel(sum_ref, raw_ref, amp_ref, out_ref, weight_ref):
        @pl.when(pl.program_id(0) == 0)
        def _():
            weights = solve(jnp.sum(sum_ref[...], axis=0, keepdims=True))
            for k in range(order):
                weight_ref[k : k + 1, :] = jnp.broadcast_to(weights[k], (1, 128))

        updated = weight_ref[count : count + 1, 0:1] * raw_ref[...]
        for k in range(count):
            updated = updated + weight_ref[k : k + 1, 0:1] * amp_ref[k].astype(f32)
        out_ref[...] = updated

    columns = lambda i: (0, i)
    return pl.pallas_call(
        kernel,
        compiler_params=small,
        grid=(width // block,),
        in_specs=[
            pl.BlockSpec(gathered.shape, lambda i: (0, 0)),
            pl.BlockSpec((rows, block), columns),
            pl.BlockSpec((count, rows, block), lambda i: (0, 0, i)),
        ],
        out_specs=pl.BlockSpec((rows, block), columns),
        out_shape=jax.ShapeDtypeStruct((rows, width), f32),
        scratch_shapes=[pltpu.VMEM((padded(order), 128), f32)],
    )(gathered, raw, hist_amp)


def cuts_of(rows):
    cuts, at = [], 0
    for part in (rows * 3 // 8, rows * 5 // 16):
        size = min(max(16, -(-part // 16) * 16), rows - at)
        if size:
            cuts.append((at, size))
        at += size
    if at < rows:
        cuts.append((at, rows - at))
    return cuts


def order_of(last):
    steps = ["p0", "n2", "p1", "f0"]
    for n in range(3, last + 1):
        steps += [f"n{n}", f"p{n - 1}"]
        steps.append("s0" if n == 3 else f"f{n - 2}")
    if last < 3:
        steps.append("s0")
    steps += [f"p{last}", "f1"]
    return steps + [f"f{n}" for n in range(max(2, last - 1), last + 1)]


def after(x, *earlier):
    return lax.optimization_barrier((x, *earlier))[0]


def make(mesh):
    row_n, col_n = mesh.shape["row"], mesh.shape["col"]
    total = row_n * col_n

    def send_col(x, m):
        return lax.ppermute(x, "col", [(i, i ^ m) for i in range(col_n)])

    def send_row(x, m):
        return lax.ppermute(x, "row", [(i, i ^ m) for i in range(row_n)])

    def on_device(
        integrals, lambda2, source_terms, hist_amp, hist_err, eps_occ, eps_vir, occ_pair, vir_pair
    ):
        rows, width = source_terms.shape
        depth = lambda2.shape[1]
        near = lambda2.shape[0] // rows
        r, c = lax.axis_index("row"), lax.axis_index("col")
        zi = r // near
        holder = lax.rem(zi, 2) == lax.rem(c, 2)
        height = -(-rows // 16) * 16

        def links_of(pair_of):
            links = []
            for z in range(col_n):
                for y in range(col_n):
                    z2 = pair_of(z, y)
                    if z2 is not None:
                        for x in range(near):
                            links.append(
                                ((z * near + x) * col_n + y, (z2 * near + x) * col_n + y)
                            )
            return links

        def multiply(piece, right):
            out = jnp.dot(
                piece.reshape(-1, depth), right, preferred_element_type=f32
            )
            return out.reshape(near, -1, width)

        def near_begin(part):
            bit = 1
            while True:
                count = part.shape[0]
                halves = part.reshape(count, part.shape[1] // 2, 2, *part.shape[2:])
                mine = (r // bit) % 2 == 0
                send = jnp.where(mine, halves[:, :, 1], halves[:, :, 0]).astype(wire)
                keep = jnp.where(mine, halves[:, :, 0], halves[:, :, 1])
                taken = send_row(send, bit)
                if keep.shape[1] == 1:
                    return keep[:, 0], taken[:, 0], send
                part = keep + taken.astype(f32)
                bit *= 2

        even_links = links_of(lambda z, y: z ^ 1 if (z ^ y) & 1 else None)

        def pair_begin(part):
            send = part.astype(wire)
            return part, lax.ppermute(send, ("row", "col"), even_links), send

        def far_begin(part, pair):
            kept = jnp.where(zi == c ^ (2 * pair), part, 0.0)
            data = part.astype(wire)
            taken = []
            for d in range(1, col_n // 2):
                links = links_of(
                    lambda z, y: z ^ (2 * d) if z ^ y ^ (2 * pair) == 2 * d else None
                )
                taken.append(lax.ppermute(data, ("row", "col"), links))
            return kept, taken, data

        def far_end(kept, taken):
            for one in taken:
                kept = kept + one.astype(f32)
            return kept

        def cut(at, size):
            parts = []
            for x in range(near):
                part = lambda2[x * rows + at : x * rows + min(at + size, rows)]
                parts.append(jnp.pad(part, ((0, size - part.shape[0]), (0, 0))))
            return jnp.stack(parts)

        cuts = cuts_of(height)
        stages = [(m, at, size) for m in range(2, col_n, 2) for at, size in cuts]
        far = {}

        def send_far(n, *earlier):
            if n < len(stages):
                m, at, size = stages[n]
                far[n] = send_col(lax.optimization_barrier((cut(at, size), *earlier))[0], m)
                return far[n]

        piece = lax.optimization_barrier(cut(*cuts[0]))
        far[0] = send_col(piece, stages[0][0])
        across = send_col(after(integrals, piece), 1)
        own = after(cut(0, height), piece)

        nears, pairs, fars = {}, {}, {}
        nears[0] = near_begin(multiply(own, integrals)[None])
        send_far(1, nears[0][2])
        across = after(across, nears[0][2])
        beside, across = product_and_hold(own.reshape(-1, depth), across)
        nears[1] = near_begin(beside.reshape(1, near, -1, width))
        send_far(2, nears[1][2])
        last = len(stages) + 1

        def to_near(n, token):
            here = after(far[n - 2], token)
            send_far(n + 1, here)
            nears[n] = near_begin(
                jnp.stack([multiply(here, integrals), multiply(here, across)])
            )
            return nears[n][2]

        def to_pair(n, token):
            keep, taken, _ = nears[n]
            pairs[n] = pair_begin(keep + after(taken, token).astype(f32))
            return pairs[n][2]

        def to_far(n, token):
            keep, taken, _ = pairs[n]
            kept = jnp.where(holder, keep, 0.0) + after(taken, token).astype(f32)
            fars[n] = far_begin(kept, stages[n - 2][0] // 2 if n >= 2 else 0)
            return fars[n][2]

        def reduce_stored(token):
            out = stored_products(after(hist_err, token))
            occ = jnp.broadcast_to(pair_energy(occ_pair, eps_occ)[:, None], (rows, 128))
            vir = pair_energy(vir_pair, eps_vir)[None, :]
            return lax.optimization_barrier((out, occ, vir))

        token = nears[1][2]
        for step in order_of(last):
            kind, n = step[0], int(step[1:])
            if kind == "s":
                stored, occ_energy, vir_energy = reduce_stored(token)
                token = stored
            else:
                token = {"n": to_near, "p": to_pair, "f": to_far}[kind](n, token)

        first = far_end(*fars[0][:2])[0]
        second = far_end(*fars[1][:2])[0]
        done = []
        for q, (at, size) in enumerate(cuts):
            mine, other = first[at : at + size], second[at : at + size]
            for p in range(q + 2, last + 1, len(cuts)):
                total_rows = far_end(*fars[p][:2])
                mine, other = mine + total_rows[0], other + total_rows[1]
            done.append((mine, other))
        ladder = jnp.concatenate(
            [mine + send_col(other, 1) for mine, other in done], axis=0
        )

        raw, shares = new_products(
            ladder, source_terms, occ_energy, vir_energy, hist_amp, hist_err, stored, total
        )
        gathered = lax.all_to_all(shares, ("row", "col"), 0, 0, tiled=True)
        return extrapolate(gathered, raw, hist_amp)

    return on_device


def solution(mesh):
    placed = (
        P("row", "col"),
        P("col", "row"),
        P("row", "col"),
        P(None, "row", "col"),
        P(None, "row", "col"),
        P(),
        P(),
        P(None, "row"),
        P(None, "col"),
    )
    return jax.shard_map(
        make(mesh), mesh=mesh, in_specs=placed, out_specs=P("row", "col"), check_vma=False
    )
```
